32 devices in a mesh: coord: 8 (over z, y), ka: 4 (over x, core).
Axes of the slice: x: 2, y: 2, z: 4, core: 2. Of those that a mesh axis runs over, the one named last changes fastest.
Arguments:
- states: float32 [4, 512, 512, 128], P('ka', 'coord'), may hold values from -6 to 6
- potential: float32 [512, 512, 128], P('coord'), may hold values from 0 to 3
- rotation_factor: float32 [512, 512], P('coord'), may hold values from 0.05 to 0.4
- basis_first: float32 [512, 512], replicated, may hold values from -0.25 to 0.25
- basis_second: float32 [512, 512], replicated, may hold values from -0.25 to 0.25
- basis_third: float32 [128, 128], replicated, may hold values from -0.5 to 0.5
- levels_first: float32 [512], replicated, may hold values from 0 to 2
- levels_second: float32 [512], replicated, may hold values from 0 to 2
- levels_third: float32 [128], replicated, may hold values from 0 to 2
- kinetic_first: float32 [512, 512], replicated, as said below
- kinetic_second: float32 [512, 512], replicated, as said below
- kinetic_third: float32 [128, 128], replicated, as said below
- coriolis_matrix: float32 [128, 128], replicated, may hold values from -0.5 to 0.5
Outputs:
- correction: float32 [4, 512, 512, 128], P('ka', 'coord')
- residual: float32 [4, 512, 512, 128], P('ka', 'coord')
The draws below stay inside these ranges and needn't reach their ends.
Inputs may be any that keep to these rules, and one draw needn't show every extreme that they name: `kinetic_first`: symmetric. `kinetic_second`: symmetric. `kinetic_third`: symmetric.
All inputs are finite; a program needn't handle non-finite values.
Results may differ from the reference program's by a relative error of at most 0.000052.
Values sent between devices are 32-bit elements; how exact they have to be, the bound alone decides.
No kernel may reach another device: no remote copies, remote signals or barrier semaphores. Data moves between devices by JAX's collectives and lax.ppermute only.
A program may use at most 256 MiB of HBM per device.

```python
import math
import jax
import jax.numpy as jnp
from jax import lax

N1 = 512
N2 = 512
N3 = 128
K_BLOCKS = 4


def symmetric_draw(key, salt, order):
    local = jax.random.fold_in(key, salt)
    entries = jax.random.uniform(local, (order, order), jnp.float32, -1.0, 1.0)
    return (entries + entries.T) * (0.5 / math.sqrt(order)) + jnp.eye(order, dtype=jnp.float32)


def draw_kinetic_first(key, part):
    return symmetric_draw(key, 11, N1)


def draw_kinetic_second(key, part):
    return symmetric_draw(key, 23, N2)


def draw_kinetic_third(key, part):
    return symmetric_draw(key, 37, N3)


def steps_of(stream_key, shape, shards, least, top_value):
    gain = 1.0
    for position, blocks in shards:
        heights = jax.random.uniform(jax.random.fold_in(jax.random.fold_in(stream_key, 6), position), (blocks,), jnp.float32, least / len(shards), top_value / len(shards))
        gain = gain * jnp.repeat(jnp.exp(heights), shape[position] // blocks).reshape((-1,) + (1,) * (len(shape) - 1 - position))
    return gain


def bell_draw(rng, shape, scale, most, pieces=(), kind=jnp.bfloat16):
    values = scale * jax.random.normal(rng, shape, jnp.float32)
    if pieces:
        values = values * steps_of(rng, shape, pieces, -0.22, 0.18)
    return jnp.clip(values, -most, most).astype(kind)


def setup_inputs(seed: int = 0) -> dict:
    arg_keys = jax.random.split(jax.random.key(seed), 14)
    states = bell_draw(arg_keys[0], (K_BLOCKS, N1, N2, N3), 1.0, 6.0, ((0, 4), (1, 8)), jnp.float32)
    potential = jnp.clip(3.0 * jax.random.uniform(arg_keys[1], (N1, N2, N3), jnp.float32) ** steps_of(arg_keys[1], (N1, N2, N3), ((0, 8),), -0.2, 0.2), 0.0, 3.0)
    rotation_factor = jnp.clip(0.05 + 0.35 * jax.random.uniform(arg_keys[2], (N1, N2), jnp.float32) ** steps_of(arg_keys[2], (N1, N2), ((0, 8),), -0.2, 0.2), 0.05, 0.4)
    basis_first = bell_draw(arg_keys[3], (N1, N1), N1 ** -0.5, 0.25, (), jnp.float32)
    basis_second = bell_draw(arg_keys[4], (N2, N2), N2 ** -0.5, 0.25, (), jnp.float32)
    basis_third = bell_draw(arg_keys[5], (N3, N3), N3 ** -0.5, 0.5, (), jnp.float32)
    levels_first = jnp.clip(jax.random.uniform(arg_keys[6], (N1,), jnp.float32, 0.0, 2.0), 0.0, 2.0)
    levels_second = jnp.clip(jax.random.uniform(arg_keys[7], (N2,), jnp.float32, 0.0, 2.0), 0.0, 2.0)
    levels_third = jnp.clip(jax.random.uniform(arg_keys[8], (N3,), jnp.float32, 0.0, 2.0), 0.0, 2.0)
    kinetic_first = draw_kinetic_first(jax.random.fold_in(arg_keys[13], 71), 0)
    kinetic_second = draw_kinetic_second(jax.random.fold_in(arg_keys[13], 71), 0)
    kinetic_third = draw_kinetic_third(jax.random.fold_in(arg_keys[13], 71), 0)
    coriolis_matrix = bell_draw(arg_keys[12], (N3, N3), N3 ** -0.5, 0.5, (), jnp.float32)
    return dict(states=states, potential=potential, rotation_factor=rotation_factor, basis_first=basis_first, basis_second=basis_second, basis_third=basis_third, levels_first=levels_first, levels_second=levels_second, levels_third=levels_third, kinetic_first=kinetic_first, kinetic_second=kinetic_second, kinetic_third=kinetic_third, coriolis_matrix=coriolis_matrix)


highest = lax.Precision.HIGHEST
shift_energy = 2.5
damping = 0.5

def settle(block, basis_first, basis_second, basis_third, filt):
    coeff = jnp.einsum('ijk,kc->ijc', block, basis_third, precision=highest)
    coeff = jnp.einsum('ijc,jb->ibc', coeff, basis_second, precision=highest)
    coeff = jnp.einsum('ibc,ia->abc', coeff, basis_first, precision=highest)
    coeff = coeff * filt
    back = jnp.einsum('ia,abc->ibc', basis_first, coeff, precision=highest)
    back = jnp.einsum('jb,ibc->ijc', basis_second, back, precision=highest)
    return jnp.einsum('kc,ijc->ijk', basis_third, back, precision=highest)

def reference(states, potential, rotation_factor, basis_first, basis_second, basis_third, levels_first, levels_second, levels_third, kinetic_first, kinetic_second, kinetic_third, coriolis_matrix):
    level = levels_first[:, None, None] + levels_second[None, :, None] + levels_third[None, None, :] - shift_energy
    filt = level / (level * level + damping * damping)

    def precondition(block):
        return settle(block, basis_first, basis_second, basis_third, filt)
    correction = lax.map(precondition, states)
    zeros = jnp.zeros_like(correction[:1])
    upper = jnp.concatenate([correction[1:], zeros], axis=0)
    lower = jnp.concatenate([zeros, correction[:-1]], axis=0)
    kvalues = jnp.arange(K_BLOCKS).astype(jnp.float32)
    square_top = (K_BLOCKS - 1) * K_BLOCKS
    factor = rotation_factor[:, :, None]

    def apply_block(items):
        source, solved, above, below, kval = items
        kinetic = jnp.einsum('im,mjk->ijk', kinetic_first, solved, precision=highest)
        kinetic = kinetic + jnp.einsum('jm,imk->ijk', kinetic_second, solved, precision=highest)
        kinetic = kinetic + jnp.einsum('km,ijm->ijk', kinetic_third, solved, precision=highest)
        coupled_up = jnp.sqrt(square_top - kval * (kval + 1.0))
        coupled_down = jnp.sqrt(square_top - (kval - 1.0) * kval)
        from_upper = jnp.einsum('km,ijm->ijk', coriolis_matrix, above, precision=highest)
        from_lower = jnp.einsum('mk,ijm->ijk', coriolis_matrix, below, precision=highest)
        coupling = factor * (coupled_up * from_upper + coupled_down * from_lower)
        applied = kinetic + (potential + kval * kval * factor) * solved + coupling
        return source - (applied - shift_energy * solved)
    residual = lax.map(apply_block, (states, correction, upper, lower, kvalues))
    return (correction, residual)
```

```python
import functools

import jax
import jax.numpy as jnp
from jax import lax
from jax.experimental import pallas as pl
from jax.experimental.pallas import tpu as pltpu
from jax.sharding import PartitionSpec as P

highest = lax.Precision.HIGHEST
high = lax.Precision.HIGH
shift_energy = 2.5
damping = 0.5
vmem_limit = 56 * 1024 * 1024


def halves(value):
    leading = lax.reduce_precision(value, 8, 7)
    return leading.astype(jnp.bfloat16), (value - leading).astype(jnp.bfloat16)


def parts(value):
    leading = value.astype(jnp.bfloat16)
    return leading, (value - leading.astype(jnp.float32)).astype(jnp.bfloat16)


def product(left, right, dims=(((1,), (0,)), ((), ()))):
    dot = functools.partial(lax.dot_general, dimension_numbers=dims, preferred_element_type=jnp.float32)
    return dot(left[0], right[0]) + (dot(left[0], right[1]) + dot(left[1], right[0]))


def whole(array):
    return pl.BlockSpec(array.shape, lambda *_: (0,) * array.ndim)


def call(kernel, grid, in_specs, out_specs, out_shape, aliases={}):
    return pl.pallas_call(
        kernel,
        grid=grid,
        in_specs=in_specs,
        out_specs=out_specs,
        out_shape=out_shape,
        input_output_aliases=aliases,
        compiler_params=pltpu.CompilerParams(vmem_limit_bytes=vmem_limit),
    )


def f32(*shape):
    return jax.ShapeDtypeStruct(shape, jnp.float32)


def third_forward(source, weights):
    rows, columns, depth = source.shape
    step = 8
    width = weights[0].shape[0]

    def kernel(source_ref, first_ref, rest_ref, out_ref):
        weight = (first_ref[...], rest_ref[...])
        for row in range(step):
            out_ref[:, row, :] = product(weight, parts(source_ref[row]), (((1,), (1,)), ((), ())))

    return call(
        kernel,
        (rows // step,),
        [pl.BlockSpec((step, columns, depth), lambda g: (g, 0, 0)), whole(weights[0]), whole(weights[1])],
        pl.BlockSpec((width, step, columns), lambda g: (0, g, 0)),
        f32(width, rows, columns),
    )(source, *weights)


def front(value, weights, start, width, own=None, far_rows=None, returned=None):
    _, rows, depth = value.shape
    half = weights[0].shape[1] // 2
    widths = [w for w in (width, own.shape[0] if own is not None else 0, returned[0].shape[0] if returned else 0) if w]
    grid = max(min(widths) // 4, 1)
    operands, in_specs, out_specs, out_shape = [], [], [], []

    def rows_of(array, index, tall=rows):
        deep = array.shape[0] // grid
        operands.append(array)
        in_specs.append(pl.BlockSpec((deep, tall, half), lambda g: (g, index, 0)))

    def result(deep, tall):
        out_specs.append(pl.BlockSpec((deep // grid, tall, half), lambda g: (g, 0, 0)))
        out_shape.append(f32(deep, tall, half))

    merged = bool(width and returned and returned[0].shape[0] == width)
    if width:
        deep = width // grid
        operands.append(value)
        in_specs.append(pl.BlockSpec((deep, rows, depth), lambda g: (start // deep + g, 0, 0)))
        for weight in weights:
            operands.append(weight)
            in_specs.append(whole(weight))
        result(width, rows)
        result(width, 3 * rows if merged else rows)
    if own is not None:
        rows_of(own, 0)
        rows_of(*far_rows)
        result(own.shape[0], 2 * rows)
    if returned:
        for array in returned:
            rows_of(array, 1, 2 * rows)
        if not merged:
            result(returned[0].shape[0], 2 * rows)

    def kernel(*refs):
        ins, outs = list(refs[: len(operands)]), list(refs[len(operands) :])
        away = None
        if width:
            value_ref, first_ref, rest_ref = ins[:3]
            del ins[:3]
            block = parts(value_ref[...].reshape(deep * rows, depth))
            out = product(block, (first_ref[...], rest_ref[...]))
            outs.pop(0)[...] = out[:, :half].reshape(deep, rows, half)
            away = outs.pop(0)
            away[:, :rows] = out[:, half:].reshape(deep, rows, half)
        if own is not None:
            both = outs.pop(0)
            both[:, :rows] = ins.pop(0)[...]
            both[:, rows:] = ins.pop(0)[...]
        if returned:
            total = ins[0][...] + ins[1][...]
            if merged:
                away[:, rows:] = total
            else:
                outs.pop(0)[...] = total

    got = list(call(kernel, (grid,), in_specs, out_specs, out_shape)(*operands))
    here = away = both = back = None
    if width:
        here, away = got.pop(0), got.pop(0)
    if own is not None:
        both = got.pop(0)
    if returned and not merged:
        back = got.pop(0)
    return here, away, both, back, merged


def centre(blocks, inward, outward, first, second, third, start):
    width, rows, columns = blocks[0].shape
    step = min(width, 4)

    def kernel(third_ref, *refs):
        block_refs = refs[: len(blocks)]
        in_first, in_rest, out_first, out_rest, first_ref, second_ref, near_ref, far_ref = refs[len(blocks) :]
        for layer in range(step):
            value = jnp.concatenate([ref[layer] for ref in block_refs], axis=0)
            coeff = product((in_first[...], in_rest[...]), parts(value))
            angle = third_ref[start + pl.program_id(0) * step + layer]
            level = first_ref[...] + second_ref[...] + angle - shift_energy
            coeff = coeff * (level / (level * level + damping * damping))
            back = product((out_first[...], out_rest[...]), parts(coeff))
            near_ref[layer] = back[: 2 * rows]
            far_ref[layer] = back[2 * rows :]

    spec = pl.BlockSpec((step, rows, columns), lambda g: (g, 0, 0))
    out_spec = pl.BlockSpec((step, 2 * rows, columns), lambda g: (g, 0, 0))
    small = (*inward, *outward, first, second)
    return call(
        kernel,
        (width // step,),
        [pl.BlockSpec(memory_space=pltpu.SMEM)] + [spec] * len(blocks) + [whole(a) for a in small],
        [out_spec, out_spec],
        [f32(width, 2 * rows, columns)] * 2,
    )(third, *blocks, *small)


def second_back(mine, other, full, weights, kinetic_weights, start, arrived=None, arrived_start=0):
    width, quad, half = mine[0].shape
    rows = quad // 4
    columns = weights[0].shape[1]
    step = min(width, 4)
    grid = width // step
    small = (*weights, *kinetic_weights)
    other, place = other
    extra = list(arrived or [])
    extra_deep = extra[0].shape[0] // grid if extra else 0

    def kernel(near_ref, returned_ref, first_other, second_other, first_ref, rest_ref, kin_first, kin_rest, *refs):
        extra_refs, outs = refs[: len(extra)], refs[len(extra) + 2 * bool(extra) + 2 :]
        total = near_ref[...] + returned_ref[...]
        block = [
            parts(
                jnp.concatenate(
                    [
                        total[:, term * rows : (term + 1) * rows, :].reshape(step * rows, half),
                        ref[...].reshape(step * rows, half),
                    ],
                    axis=1,
                )
            )
            for term, ref in enumerate((first_other, second_other))
        ]
        weight = (first_ref[...], rest_ref[...])
        solved = product(block[0], weight).reshape(step, rows, columns)
        outs[0][...] = solved
        outs[1][...] = solved
        kinetic = product(block[1], weight) + product(block[0], (kin_first[...], kin_rest[...]))
        outs[2][...] = kinetic.reshape(step, rows, columns)
        for ref, out in zip(extra_refs, outs[3:]):
            out[...] = ref[...]

    def layers(deep, first):
        return pl.BlockSpec((deep, rows, columns), lambda g: (first // deep + g, 0, 0))

    def rows_at(index, tall):
        return pl.BlockSpec((step, tall, half), lambda g: (g, index, 0))

    kept = list(full if extra else full[:2])
    operands = [*mine, other, other, *small, *extra, *kept]
    first_kept = len(operands) - len(kept)
    got = call(
        kernel,
        (grid,),
        [rows_at(0, 2 * rows)] * 2
        + [rows_at(place, rows), rows_at(place + 1, rows)]
        + [whole(a) for a in small]
        + [layers(extra_deep, 0)] * len(extra)
        + [pl.BlockSpec(memory_space=pl.ANY)] * len(kept),
        [layers(step, 0)] + [layers(step, start)] * 2 + ([layers(extra_deep, arrived_start)] * 2 if extra else []),
        [f32(width, rows, columns)] + [f32(*a.shape) for a in kept],
        {first_kept + n: 1 + n for n in range(len(kept))},
    )(*operands)
    return got[0], tuple(got[1:]) + tuple(full[len(kept) :])


def third_back(solved, kinetic, even, odd, source, potential, rotation, weights, coupling_weights, square):
    depth, rows, columns = solved.shape
    width = source.shape[2]
    step = 8

    def kernel(square_ref, solved_ref, kinetic_ref, even_ref, odd_ref, source_ref, potential_ref, rotation_ref, *refs):
        first_ref, rest_ref, mix_first, mix_rest, out_ref, residual_ref = refs
        weight = (first_ref[...], rest_ref[...])
        mix = (mix_first[...], mix_rest[...])
        for row in range(step):
            both = product(
                weight, parts(jnp.concatenate([solved_ref[:, row, :], kinetic_ref[:, row, :]], axis=0))
            )
            coupled = product(mix, parts(jnp.concatenate([even_ref[:, row, :], odd_ref[:, row, :]], axis=0)))
            upper, lower = both[:width], both[width:]
            factor = rotation_ref[row : row + 1, :]
            lower = lower + factor * (coupled + square_ref[0, 0] * upper) - shift_energy * upper
            upper, lower = upper.T, lower.T
            out_ref[row] = upper
            residual_ref[row] = source_ref[row] - (lower + potential_ref[row] * upper)

    layer = pl.BlockSpec((depth, step, columns), lambda g: (0, g, 0))
    slab = pl.BlockSpec((step, columns, width), lambda g: (g, 0, 0))
    small = (*weights, *coupling_weights)
    return call(
        kernel,
        (rows // step,),
        [pl.BlockSpec(memory_space=pltpu.SMEM)]
        + [layer] * 4
        + [slab] * 2
        + [pl.BlockSpec((step, columns), lambda g: (g, 0))]
        + [whole(a) for a in small],
        [slab, slab],
        [f32(*source.shape)] * 2,
    )(square, solved, kinetic, even, odd, source, potential, rotation, *small)


def unwritten(shape, count):
    def kernel(*refs):
        pass

    anywhere = pl.BlockSpec(memory_space=pl.ANY)
    return pl.pallas_call(kernel, out_specs=[anywhere] * count, out_shape=[f32(*shape)] * count)()


def chunk_widths(total):
    unit = total // 16
    small = unit // 2
    return [small] * 2 + [unit] * 13 + [small] * 4


def line_plan(
    states,
    potential,
    rotation_factor,
    basis_first,
    basis_second,
    basis_third,
    levels_first,
    levels_second,
    levels_third,
    kinetic_first,
    kinetic_second,
    kinetic_third,
    coriolis_matrix,
):
    source = states[0]
    count = lax.axis_size("coord")
    blocks = lax.axis_size("ka")
    coord = lax.axis_index("coord")
    kindex = lax.axis_index("ka")
    layer, side = coord // 2, coord % 2
    layers = count // 2
    rows, second_size, third_size = source.shape
    first_size = basis_first.shape[0]
    half = second_size // 2
    dot = functools.partial(jnp.dot, precision=highest)

    def place(z, y):
        return 2 * z + y

    sides = range(2)
    inner = (layers // 2 - 1, layers // 2)
    to_inner = [(place(z ^ 1, y), place(z, y)) for z in inner for y in sides]
    to_outer = [(b, a) for a, b in to_inner]
    across = [(place(z, y), place(layers - 1 - z, y)) for z in inner for y in sides]
    facing_side = [(place(z, y), place(z, 1 - y)) for z in range(layers) for y in sides]
    even_pairs = [pair for k in range(0, blocks - 1, 2) for pair in ((k, k + 1), (k + 1, k))]
    odd_pairs = [pair for k in range(1, blocks - 1, 2) for pair in ((k, k + 1), (k + 1, k))]

    def mine_first(matrix, axis):
        return jnp.roll(matrix, -side * half, axis)

    weights_third = halves(basis_third.T)
    layered = third_forward(source, weights_third)
    basis_mine = mine_first(basis_second, 1)
    weights_second = halves(basis_mine)

    def prepare(gate):
        tied = lax.optimization_barrier((gate, basis_first, basis_mine, basis_third, kinetic_first))
        gate, first, second, third, kin_first = tied
        kinetic_basis = dot(kin_first, first)
        is_inner = jnp.logical_and(layer >= inner[0], layer <= inner[1]).astype(jnp.float32)

        def block(matrix, z, y):
            return lax.dynamic_slice_in_dim(matrix, (2 * z + y) * rows, rows)

        pair_layer = layer ^ 1
        facing = layers - 1 - layer
        both_sides = (side, 1 - side)
        order = [(z, y) for z in (layer, pair_layer, facing, facing ^ 1) for y in both_sides]
        inward = jnp.concatenate([block(first, z, y) for z, y in order], axis=0).T
        near = jnp.concatenate([block(m, layer, y) for y in both_sides for m in (first, kinetic_basis)], axis=0)
        far = jnp.concatenate([block(m, pair_layer, y) for y in both_sides for m in (first, kinetic_basis)], axis=0)
        outward = jnp.concatenate([near * is_inner, far], axis=0)
        turned = second.T
        kinetic_turned = dot(kinetic_second, second).T
        kval = kindex.astype(jnp.float32)
        square_top = (blocks - 1) * blocks
        coupled_up = jnp.sqrt(square_top - kval * (kval + 1.0))
        coupled_down = jnp.sqrt(square_top - (kval - 1.0) * kval)
        up = coupled_up * dot(coriolis_matrix, third)
        down = coupled_down * dot(coriolis_matrix.T, third)
        is_even = kindex % 2 == 0
        mix = jnp.concatenate([jnp.where(is_even, up, down), jnp.where(is_even, down, up)], axis=1)
        both = jnp.concatenate(
            [
                jnp.concatenate([third, jnp.zeros_like(third)], axis=1),
                jnp.concatenate([dot(kinetic_third, third), third], axis=1),
            ],
            axis=0,
        )
        return gate, dict(
            inward=halves(inward),
            outward=halves(outward),
            turned=halves(turned),
            kinetic_turned=halves(kinetic_turned),
            both=halves(both),
            mix=halves(mix),
            square=(kval * kval).reshape(1, 1),
            first=levels_first[:, None],
            second=lax.dynamic_slice_in_dim(levels_second, side * half, half)[None, :],
        )

    widths = chunk_widths(third_size)
    starts = [sum(widths[:q]) for q in range(len(widths))]
    total = len(widths)
    full = unwritten((third_size, rows, second_size), 4)

    ready, sent, place_back, table = {}, {}, {}, None
    for step in range(-2, total + 6):

        def live(q):
            return 0 <= q < total

        q = step
        if live(q):
            ready["relay", q] = lax.ppermute(ready["outer", q], "coord", across)
        q = step - 1
        if live(q):
            sent["returned", q] = lax.ppermute(ready.pop(("far", q)), "coord", to_outer)
        ahead, arrived, behind = step + 2, step + 1, step - 3
        if live(ahead) or live(arrived) or live(behind):
            pair = None
            if live(behind):
                pair = ready["returned", behind] = (ready.pop(("near", behind)), sent.pop(("returned", behind)))
            here, away, both, back, merged = front(
                layered,
                weights_second,
                starts[ahead] if live(ahead) else 0,
                widths[ahead] if live(ahead) else 0,
                ready.pop(("here", arrived), None),
                (ready.pop(("rows in", arrived)), 0) if live(arrived) else None,
                pair,
            )
            if live(arrived):
                ready["own", arrived] = both
            if away is not None:
                away = lax.ppermute(away, "coord", facing_side)
                ready["here", ahead], ready["rows in", ahead] = here, away
            if merged:
                ready["rows back", behind] = away
                place_back[behind] = 1
            elif back is not None:
                ready["rows back", behind] = lax.ppermute(back, "coord", facing_side)
        q = step + 1
        if live(q):
            sent["facing", q] = lax.ppermute(ready["own", q], "coord", across)
            ready["outer", q] = lax.ppermute(ready["own", q], "coord", to_inner)
        if step == -1:
            ready["own", 0], table = prepare(ready["own", 0])
        q = step - 4
        if live(q):
            late = q - 2
            solved, full = second_back(
                ready.pop(("returned", q)),
                (ready.pop(("rows back", q)), place_back.get(q, 0)),
                full,
                table["turned"],
                table["kinetic_turned"],
                starts[q],
                [ready.pop(("even", late)), ready.pop(("odd", late))] if live(late) else None,
                starts[late] if live(late) else 0,
            )
            ready["even", q] = lax.ppermute(solved, "ka", even_pairs)
            ready["odd", q] = lax.ppermute(solved, "ka", odd_pairs)
        q = step
        if live(q):
            together = (ready.pop(("own", q)), ready.pop(("outer", q)), sent.pop(("facing", q)), ready.pop(("relay", q)))
            ready["near", q], ready["far", q] = centre(
                together, table["inward"], table["outward"], table["first"], table["second"], levels_third, starts[q]
            )
        (layered, full), ready = lax.optimization_barrier(((layered, full), ready))
    full = list(full)
    for q in range(total):
        for place_of, name in ((2, "even"), (3, "odd")):
            if (name, q) in ready:
                full[place_of] = lax.dynamic_update_slice(full[place_of], ready.pop((name, q)), (starts[q], 0, 0))
    solved_full, kinetic_full, even_full, odd_full = full

    solved, residual = third_back(
        solved_full,
        kinetic_full,
        even_full,
        odd_full,
        source,
        potential,
        rotation_factor,
        table["both"],
        table["mix"],
        table["square"],
    )
    return (solved[None], residual[None])


def from_behind(value, axis, steps):
    count = lax.axis_size(axis)
    leading, last = (max(0, -steps), min(count, count - steps))
    return lax.ppermute(value, axis, [(source, source + steps) for source in range(leading, last)])


def finish_slab(back, basis_second, basis_third):
    back = jnp.einsum("jb,ibc->ijc", basis_second, back, precision=high)
    return jnp.einsum("kc,ijc->ijk", basis_third, back, precision=high)


def column_plan(
    states,
    potential,
    rotation_factor,
    basis_first,
    basis_second,
    basis_third,
    levels_first,
    levels_second,
    levels_third,
    kinetic_first,
    kinetic_second,
    kinetic_third,
    coriolis_matrix,
):
    source = states[0]
    coeff = jnp.einsum("ijk,kc->ijc", source, basis_third, precision=high)
    coeff = jnp.einsum("ijc,jb->ibc", coeff, basis_second, precision=high)
    columns = lax.all_to_all(coeff, "coord", split_axis=1, concat_axis=0, tiled=True)
    width = columns.shape[1]
    start = lax.axis_index("coord") * width
    local_second = lax.dynamic_slice_in_dim(levels_second, start, width)
    level = (
        levels_first[:, None, None]
        + local_second[None, :, None]
        + levels_third[None, None, :]
        - shift_energy
    )
    filt = level / (level * level + damping * damping)
    columns = jnp.einsum("ibc,ia->abc", columns, basis_first, precision=high)
    columns = columns * filt
    back = jnp.einsum("ia,abc->ibc", basis_first, columns, precision=high)
    kinetic_back = jnp.einsum("im,mbc->ibc", kinetic_first, back, precision=high)
    back_rows, kinetic_rows = (
        lax.all_to_all(back, "coord", split_axis=0, concat_axis=1, tiled=True),
        lax.all_to_all(kinetic_back, "coord", split_axis=0, concat_axis=1, tiled=True),
    )
    solved = finish_slab(back_rows, basis_second, basis_third)
    kinetic = finish_slab(kinetic_rows, basis_second, basis_third)
    above = from_behind(solved, "ka", -1)
    below = from_behind(solved, "ka", 1)
    kinetic = kinetic + jnp.einsum("jm,imk->ijk", kinetic_second, solved, precision=high)
    kinetic = kinetic + jnp.einsum("km,ijm->ijk", kinetic_third, solved, precision=high)
    kval = lax.axis_index("ka").astype(jnp.float32)
    blocks = lax.axis_size("ka")
    square_top = (blocks - 1) * blocks
    coupled_up = jnp.sqrt(square_top - kval * (kval + 1.0))
    coupled_down = jnp.sqrt(square_top - (kval - 1.0) * kval)
    factor = rotation_factor[:, :, None]
    from_upper = jnp.einsum("km,ijm->ijk", coriolis_matrix, above, precision=high)
    from_lower = jnp.einsum("mk,ijm->ijk", coriolis_matrix, below, precision=high)
    coupling = factor * (coupled_up * from_upper + coupled_down * from_lower)
    applied = kinetic + (potential + kval * kval * factor) * solved + coupling
    residual = source - (applied - shift_energy * solved)
    return (solved[None], residual[None])


def solution(mesh):
    layers = mesh.shape["coord"] // 2
    plan = line_plan if layers == 4 else column_plan
    return jax.shard_map(
        plan,
        mesh=mesh,
        in_specs=(
            P("ka", "coord", None, None),
            P("coord", None, None),
            P("coord", None),
            P(),
            P(),
            P(),
            P(),
            P(),
            P(),
            P(),
            P(),
            P(),
            P(),
        ),
        out_specs=(P("ka", "coord", None, None), P("ka", "coord", None, None)),
        check_vma=False,
    )
```

```python
import functools

import jax
import jax.numpy as jnp
from jax import lax
from jax.experimental import pallas as pl
from jax.experimental.pallas import tpu as pltpu
from jax.sharding import PartitionSpec as P

highest = lax.Precision.HIGHEST
high = lax.Precision.HIGH
shift_energy = 2.5
damping = 0.5
vmem_limit = 56 * 1024 * 1024


def halves(value):
    leading = lax.reduce_precision(value, 8, 7)
    return leading.astype(jnp.bfloat16), (value - leading).astype(jnp.bfloat16)


def parts(value):
    leading = value.astype(jnp.bfloat16)
    return leading, (value - leading.astype(jnp.float32)).astype(jnp.bfloat16)


def product(left, right, dims=(((1,), (0,)), ((), ()))):
    dot = functools.partial(lax.dot_general, dimension_numbers=dims, preferred_element_type=jnp.float32)
    return dot(left[0], right[0]) + (dot(left[0], right[1]) + dot(left[1], right[0]))


def whole(array):
    return pl.BlockSpec(array.shape, lambda *_: (0,) * array.ndim)


def call(kernel, grid, in_specs, out_specs, out_shape, aliases={}):
    return pl.pallas_call(
        kernel,
        grid=grid,
        in_specs=in_specs,
        out_specs=out_specs,
        out_shape=out_shape,
        input_output_aliases=aliases,
        compiler_params=pltpu.CompilerParams(vmem_limit_bytes=vmem_limit),
    )


def f32(*shape):
    return jax.ShapeDtypeStruct(shape, jnp.float32)


def third_forward(source, weights):
    rows, columns, depth = source.shape
    step = 8
    width = weights[0].shape[0]

    def kernel(source_ref, first_ref, rest_ref, out_ref):
        weight = (first_ref[...], rest_ref[...])
        for row in range(step):
            out_ref[:, row, :] = product(weight, parts(source_ref[row]), (((1,), (1,)), ((), ())))

    return call(
        kernel,
        (rows // step,),
        [pl.BlockSpec((step, columns, depth), lambda g: (g, 0, 0)), whole(weights[0]), whole(weights[1])],
        pl.BlockSpec((width, step, columns), lambda g: (0, g, 0)),
        f32(width, rows, columns),
    )(source, *weights)


def front(value, weights, start, width, own=None, far_rows=None, layers=None, returned=None):
    _, rows, depth = value.shape
    half = weights[0].shape[1] // 2
    widths = [width or None] + [group[0].shape[0] for group in (far_rows, layers, returned) if group]
    grid = max(min(w for w in widths if w) // 4, 1)
    operands, in_specs, out_specs, out_shape = [], [], [], []

    def rows_of(array, index, tall=rows):
        deep = array.shape[0] // grid
        operands.append(array)
        in_specs.append(pl.BlockSpec((deep, tall, half), lambda g: (g, index, 0)))

    def result(deep, tall):
        out_specs.append(pl.BlockSpec((deep // grid, tall, half), lambda g: (g, 0, 0)))
        out_shape.append(f32(deep, tall, half))

    merged = bool(width and returned and returned[0].shape[0] == width)
    if width:
        deep = width // grid
        operands.append(value)
        in_specs.append(pl.BlockSpec((deep, rows, depth), lambda g: (start // deep + g, 0, 0)))
        for weight in weights:
            operands.append(weight)
            in_specs.append(whole(weight))
        result(width, rows)
        result(width, 3 * rows if merged else rows)
    if own is not None:
        rows_of(own, 0)
        rows_of(*far_rows)
        result(own.shape[0], 2 * rows)
    if layers:
        for array in layers:
            rows_of(array, 0, 2 * rows)
        result(layers[0].shape[0], 4 * rows)
    if returned:
        for array in returned:
            rows_of(array, 1, 2 * rows)
        if not merged:
            result(returned[0].shape[0], 2 * rows)

    def kernel(*refs):
        ins, outs = list(refs[: len(operands)]), list(refs[len(operands) :])
        away = None
        if width:
            value_ref, first_ref, rest_ref = ins[:3]
            del ins[:3]
            block = parts(value_ref[...].reshape(deep * rows, depth))
            out = product(block, (first_ref[...], rest_ref[...]))
            outs.pop(0)[...] = out[:, :half].reshape(deep, rows, half)
            away = outs.pop(0)
            away[:, :rows] = out[:, half:].reshape(deep, rows, half)
        if own is not None:
            both = outs.pop(0)
            both[:, :rows] = ins.pop(0)[...]
            both[:, rows:] = ins.pop(0)[...]
        if layers:
            across = outs.pop(0)
            across[:, : 2 * rows] = ins.pop(0)[...]
            across[:, 2 * rows :] = ins.pop(0)[...]
        if returned:
            total = ins[0][...] + ins[1][...]
            if merged:
                away[:, rows:] = total
            else:
                outs.pop(0)[...] = total

    got = list(call(kernel, (grid,), in_specs, out_specs, out_shape)(*operands))
    here = away = both = across = back = None
    if width:
        here, away = got.pop(0), got.pop(0)
    if own is not None:
        both = got.pop(0)
    if layers:
        across = got.pop(0)
    if returned and not merged:
        back = got.pop(0)
    return here, away, both, across, back, merged


def centre(blocks, inward, outward, first, second, third, start):
    width, rows, columns = blocks[0].shape
    rows //= 2
    step = min(width, 4)

    def kernel(third_ref, *refs):
        block_refs = refs[: len(blocks)]
        in_first, in_rest, out_first, out_rest, first_ref, second_ref, near_ref, far_ref = refs[len(blocks) :]
        for layer in range(step):
            value = jnp.concatenate([ref[layer] for ref in block_refs], axis=0)
            coeff = product((in_first[...], in_rest[...]), parts(value))
            angle = third_ref[start + pl.program_id(0) * step + layer]
            level = first_ref[...] + second_ref[...] + angle - shift_energy
            coeff = coeff * (level / (level * level + damping * damping))
            back = product((out_first[...], out_rest[...]), parts(coeff))
            near_ref[layer] = back[: 2 * rows]
            far_ref[layer] = back[2 * rows :]

    spec = pl.BlockSpec((step, 2 * rows, columns), lambda g: (g, 0, 0))
    small = (*inward, *outward, first, second)
    return call(
        kernel,
        (width // step,),
        [pl.BlockSpec(memory_space=pltpu.SMEM)] + [spec] * len(blocks) + [whole(a) for a in small],
        [spec, spec],
        [f32(width, 2 * rows, columns)] * 2,
    )(third, *blocks, *small)


def second_back(mine, other, full, weights, kinetic_weights, start, arrived=None, arrived_start=0):
    width, quad, half = mine[0].shape
    rows = quad // 4
    columns = weights[0].shape[1]
    step = min(width, 4)
    grid = width // step
    small = (*weights, *kinetic_weights)
    other, place = other
    extra = list(arrived or [])
    extra_deep = extra[0].shape[0] // grid if extra else 0

    def kernel(near_ref, returned_ref, first_other, second_other, first_ref, rest_ref, kin_first, kin_rest, *refs):
        extra_refs, outs = refs[: len(extra)], refs[len(extra) + 2 * bool(extra) + 2 :]
        total = near_ref[...] + returned_ref[...]
        block = [
            parts(
                jnp.concatenate(
                    [
                        total[:, term * rows : (term + 1) * rows, :].reshape(step * rows, half),
                        ref[...].reshape(step * rows, half),
                    ],
                    axis=1,
                )
            )
            for term, ref in enumerate((first_other, second_other))
        ]
        weight = (first_ref[...], rest_ref[...])
        solved = product(block[0], weight).reshape(step, rows, columns)
        outs[0][...] = solved
        outs[1][...] = solved
        kinetic = product(block[1], weight) + product(block[0], (kin_first[...], kin_rest[...]))
        outs[2][...] = kinetic.reshape(step, rows, columns)
        for ref, out in zip(extra_refs, outs[3:]):
            out[...] = ref[...]

    def layers(deep, first):
        return pl.BlockSpec((deep, rows, columns), lambda g: (first // deep + g, 0, 0))

    def rows_at(index, tall):
        return pl.BlockSpec((step, tall, half), lambda g: (g, index, 0))

    kept = list(full if extra else full[:2])
    operands = [*mine, other, other, *small, *extra, *kept]
    first_kept = len(operands) - len(kept)
    got = call(
        kernel,
        (grid,),
        [rows_at(0, 2 * rows)] * 2
        + [rows_at(place, rows), rows_at(place + 1, rows)]
        + [whole(a) for a in small]
        + [layers(extra_deep, 0)] * len(extra)
        + [pl.BlockSpec(memory_space=pl.ANY)] * len(kept),
        [layers(step, 0)] + [layers(step, start)] * 2 + ([layers(extra_deep, arrived_start)] * 2 if extra else []),
        [f32(width, rows, columns)] + [f32(*a.shape) for a in kept],
        {first_kept + n: 1 + n for n in range(len(kept))},
    )(*operands)
    return got[0], tuple(got[1:]) + tuple(full[len(kept) :])


def third_back(solved, kinetic, even, odd, source, potential, rotation, weights, coupling_weights, square):
    depth, rows, columns = solved.shape
    width = source.shape[2]
    step = 8

    def kernel(square_ref, solved_ref, kinetic_ref, even_ref, odd_ref, source_ref, potential_ref, rotation_ref, *refs):
        first_ref, rest_ref, mix_first, mix_rest, out_ref, residual_ref = refs
        weight = (first_ref[...], rest_ref[...])
        mix = (mix_first[...], mix_rest[...])
        for row in range(step):
            both = product(
                weight, parts(jnp.concatenate([solved_ref[:, row, :], kinetic_ref[:, row, :]], axis=0))
            )
            coupled = product(mix, parts(jnp.concatenate([even_ref[:, row, :], odd_ref[:, row, :]], axis=0)))
            upper, lower = both[:width], both[width:]
            factor = rotation_ref[row : row + 1, :]
            lower = lower + factor * (coupled + square_ref[0, 0] * upper) - shift_energy * upper
            upper, lower = upper.T, lower.T
            out_ref[row] = upper
            residual_ref[row] = source_ref[row] - (lower + potential_ref[row] * upper)

    layer = pl.BlockSpec((depth, step, columns), lambda g: (0, g, 0))
    slab = pl.BlockSpec((step, columns, width), lambda g: (g, 0, 0))
    small = (*weights, *coupling_weights)
    return call(
        kernel,
        (rows // step,),
        [pl.BlockSpec(memory_space=pltpu.SMEM)]
        + [layer] * 4
        + [slab] * 2
        + [pl.BlockSpec((step, columns), lambda g: (g, 0))]
        + [whole(a) for a in small],
        [slab, slab],
        [f32(*source.shape)] * 2,
    )(square, solved, kinetic, even, odd, source, potential, rotation, *small)


def unwritten(shape, count):
    def kernel(*refs):
        pass

    anywhere = pl.BlockSpec(memory_space=pl.ANY)
    return pl.pallas_call(kernel, out_specs=[anywhere] * count, out_shape=[f32(*shape)] * count)()


def chunk_widths(total):
    unit = total // 16
    small = unit // 2
    return [small] * 2 + [unit] * 15


def line_plan(
    states,
    potential,
    rotation_factor,
    basis_first,
    basis_second,
    basis_third,
    levels_first,
    levels_second,
    levels_third,
    kinetic_first,
    kinetic_second,
    kinetic_third,
    coriolis_matrix,
):
    source = states[0]
    count = lax.axis_size("coord")
    blocks = lax.axis_size("ka")
    coord = lax.axis_index("coord")
    kindex = lax.axis_index("ka")
    layer, side = coord // 2, coord % 2
    layers = count // 2
    rows, second_size, third_size = source.shape
    first_size = basis_first.shape[0]
    half = second_size // 2
    dot = functools.partial(jnp.dot, precision=highest)

    def place(z, y):
        return 2 * z + y

    sides = range(2)
    inner = (layers // 2 - 1, layers // 2)
    to_inner = [(place(z ^ 1, y), place(z, y)) for z in inner for y in sides]
    to_outer = [(b, a) for a, b in to_inner]
    across_middle = [(place(z, y), place(layers - 1 - z, y)) for z in inner for y in sides]
    facing_side = [(place(z, y), place(z, 1 - y)) for z in range(layers) for y in sides]
    even_pairs = [pair for k in range(0, blocks - 1, 2) for pair in ((k, k + 1), (k + 1, k))]
    odd_pairs = [pair for k in range(1, blocks - 1, 2) for pair in ((k, k + 1), (k + 1, k))]

    def mine_first(matrix, axis):
        return jnp.roll(matrix, -side * half, axis)

    weights_third = halves(basis_third.T)
    layered = third_forward(source, weights_third)
    basis_mine = mine_first(basis_second, 1)
    weights_second = halves(basis_mine)

    def prepare(gate):
        tied = lax.optimization_barrier((gate, basis_first, basis_mine, basis_third, kinetic_first))
        gate, first, second, third, kin_first = tied
        kinetic_basis = dot(kin_first, first)
        is_inner = jnp.logical_and(layer >= inner[0], layer <= inner[1]).astype(jnp.float32)

        def block(matrix, z, y):
            return lax.dynamic_slice_in_dim(matrix, (2 * z + y) * rows, rows)

        pair_layer = layer ^ 1
        facing = layers - 1 - layer
        both_sides = (side, 1 - side)
        order = [(z, y) for z in (layer, pair_layer, facing, facing ^ 1) for y in both_sides]
        inward = jnp.concatenate([block(first, z, y) for z, y in order], axis=0).T
        near = jnp.concatenate([block(m, layer, y) for y in both_sides for m in (first, kinetic_basis)], axis=0)
        far = jnp.concatenate([block(m, pair_layer, y) for y in both_sides for m in (first, kinetic_basis)], axis=0)
        outward = jnp.concatenate([near * is_inner, far], axis=0)
        turned = second.T
        kinetic_turned = dot(kinetic_second, second).T
        kval = kindex.astype(jnp.float32)
        square_top = (blocks - 1) * blocks
        coupled_up = jnp.sqrt(square_top - kval * (kval + 1.0))
        coupled_down = jnp.sqrt(square_top - (kval - 1.0) * kval)
        up = coupled_up * dot(coriolis_matrix, third)
        down = coupled_down * dot(coriolis_matrix.T, third)
        is_even = kindex % 2 == 0
        mix = jnp.concatenate([jnp.where(is_even, up, down), jnp.where(is_even, down, up)], axis=1)
        both = jnp.concatenate(
            [
                jnp.concatenate([third, jnp.zeros_like(third)], axis=1),
                jnp.concatenate([dot(kinetic_third, third), third], axis=1),
            ],
            axis=0,
        )
        return gate, dict(
            inward=halves(inward),
            outward=halves(outward),
            turned=halves(turned),
            kinetic_turned=halves(kinetic_turned),
            both=halves(both),
            mix=halves(mix),
            square=(kval * kval).reshape(1, 1),
            first=levels_first[:, None],
            second=lax.dynamic_slice_in_dim(levels_second, side * half, half)[None, :],
        )

    widths = chunk_widths(third_size)
    starts = [sum(widths[:q]) for q in range(len(widths))]
    total = len(widths)
    full = unwritten((third_size, rows, second_size), 4)

    ready, place_back, table = {}, {}, None
    for step in range(total + 12):
        made = {}
        chunk = [step - stage for stage in range(13)]
        live = [0 <= q < total for q in chunk]

        def send(name, key, axis, pairs):
            made[key] = lax.ppermute(ready[name], axis, pairs)

        if live[5]:
            send(("layers", chunk[5]), ("facing", chunk[5]), "coord", across_middle)
        if live[7]:
            send(("far", chunk[7]), ("returned", chunk[7]), "coord", to_outer)
        if live[3]:
            send(("own", chunk[3]), ("outer", chunk[3]), "coord", to_inner)
        if live[1]:
            send(("away", chunk[1]), ("rows in", chunk[1]), "coord", facing_side)
        if live[9]:
            q = chunk[9]
            if ("back", q) in ready:
                send(("back", q), ("rows back", q), "coord", facing_side)
                place_back[q] = 0
            else:
                made["rows back", q] = made["rows in", chunk[1]]
                place_back[q] = 1
        if live[11]:
            send(("solved", chunk[11]), ("even", chunk[11]), "ka", even_pairs)
            send(("solved", chunk[11]), ("odd", chunk[11]), "ka", odd_pairs)

        if any(live[stage] for stage in (0, 2, 4, 8)):
            here, away, both, layers_rows, back, merged = front(
                layered,
                weights_second,
                starts[chunk[0]] if live[0] else 0,
                widths[chunk[0]] if live[0] else 0,
                ready["here", chunk[2]] if live[2] else None,
                (ready["rows in", chunk[2]], 0) if live[2] else None,
                (ready["own", chunk[4]], ready["outer", chunk[4]]) if live[4] else None,
                (ready["near", chunk[8]], ready["returned", chunk[8]]) if live[8] else None,
            )
            if live[0]:
                made["here", chunk[0]], made["away", chunk[0]] = here, away
            if live[2]:
                made["own", chunk[2]] = both
            if live[4]:
                made["layers", chunk[4]] = layers_rows
            if live[8] and not merged:
                made["back", chunk[8]] = back
        if step == 1:
            ready["away", 0], table = prepare(ready["away", 0])
        if live[10]:
            q, late = chunk[10], chunk[12]
            made["solved", q], full = second_back(
                (ready["near", q], ready["returned", q]),
                (ready["rows back", q], place_back[q]),
                full,
                table["turned"],
                table["kinetic_turned"],
                starts[q],
                [ready["even", late], ready["odd", late]] if live[12] else None,
                starts[late] if live[12] else 0,
            )
        elif live[12]:
            q, full = chunk[12], list(full)
            for slot, name in ((2, "even"), (3, "odd")):
                full[slot] = lax.dynamic_update_slice(full[slot], ready[name, q], (starts[q], 0, 0))
            full = tuple(full)
        if live[6]:
            q = chunk[6]
            made["near", q], made["far", q] = centre(
                (ready["layers", q], ready["facing", q]),
                table["inward"],
                table["outward"],
                table["first"],
                table["second"],
                levels_third,
                starts[q],
            )
        last_use = {
            "here": 2,
            "away": 1,
            "rows in": 2,
            "own": 4,
            "outer": 4,
            "layers": 6,
            "facing": 6,
            "near": 10,
            "far": 7,
            "returned": 10,
            "back": 9,
            "rows back": 10,
            "solved": 11,
            "even": 12,
            "odd": 12,
        }
        ready = {key: array for key, array in ready.items() if step - key[1] < last_use[key[0]]}
        ready.update(made)
        (layered, full), ready = lax.optimization_barrier(((layered, full), ready))
    full = list(full)
    for q in range(total):
        for place_of, name in ((2, "even"), (3, "odd")):
            if (name, q) in ready:
                full[place_of] = lax.dynamic_update_slice(full[place_of], ready.pop((name, q)), (starts[q], 0, 0))
    solved_full, kinetic_full, even_full, odd_full = full

    solved, residual = third_back(
        solved_full,
        kinetic_full,
        even_full,
        odd_full,
        source,
        potential,
        rotation_factor,
        table["both"],
        table["mix"],
        table["square"],
    )
    return (solved[None], residual[None])


def from_behind(value, axis, steps):
    count = lax.axis_size(axis)
    leading, last = (max(0, -steps), min(count, count - steps))
    return lax.ppermute(value, axis, [(source, source + steps) for source in range(leading, last)])


def finish_slab(back, basis_second, basis_third):
    back = jnp.einsum("jb,ibc->ijc", basis_second, back, precision=high)
    return jnp.einsum("kc,ijc->ijk", basis_third, back, precision=high)


def column_plan(
    states,
    potential,
    rotation_factor,
    basis_first,
    basis_second,
    basis_third,
    levels_first,
    levels_second,
    levels_third,
    kinetic_first,
    kinetic_second,
    kinetic_third,
    coriolis_matrix,
):
    source = states[0]
    coeff = jnp.einsum("ijk,kc->ijc", source, basis_third, precision=high)
    coeff = jnp.einsum("ijc,jb->ibc", coeff, basis_second, precision=high)
    columns = lax.all_to_all(coeff, "coord", split_axis=1, concat_axis=0, tiled=True)
    width = columns.shape[1]
    start = lax.axis_index("coord") * width
    local_second = lax.dynamic_slice_in_dim(levels_second, start, width)
    level = (
        levels_first[:, None, None]
        + local_second[None, :, None]
        + levels_third[None, None, :]
        - shift_energy
    )
    filt = level / (level * level + damping * damping)
    columns = jnp.einsum("ibc,ia->abc", columns, basis_first, precision=high)
    columns = columns * filt
    back = jnp.einsum("ia,abc->ibc", basis_first, columns, precision=high)
    kinetic_back = jnp.einsum("im,mbc->ibc", kinetic_first, back, precision=high)
    back_rows, kinetic_rows = (
        lax.all_to_all(back, "coord", split_axis=0, concat_axis=1, tiled=True),
        lax.all_to_all(kinetic_back, "coord", split_axis=0, concat_axis=1, tiled=True),
    )
    solved = finish_slab(back_rows, basis_second, basis_third)
    kinetic = finish_slab(kinetic_rows, basis_second, basis_third)
    above = from_behind(solved, "ka", -1)
    below = from_behind(solved, "ka", 1)
    kinetic = kinetic + jnp.einsum("jm,imk->ijk", kinetic_second, solved, precision=high)
    kinetic = kinetic + jnp.einsum("km,ijm->ijk", kinetic_third, solved, precision=high)
    kval = lax.axis_index("ka").astype(jnp.float32)
    blocks = lax.axis_size("ka")
    square_top = (blocks - 1) * blocks
    coupled_up = jnp.sqrt(square_top - kval * (kval + 1.0))
    coupled_down = jnp.sqrt(square_top - (kval - 1.0) * kval)
    factor = rotation_factor[:, :, None]
    from_upper = jnp.einsum("km,ijm->ijk", coriolis_matrix, above, precision=high)
    from_lower = jnp.einsum("mk,ijm->ijk", coriolis_matrix, below, precision=high)
    coupling = factor * (coupled_up * from_upper + coupled_down * from_lower)
    applied = kinetic + (potential + kval * kval * factor) * solved + coupling
    residual = source - (applied - shift_energy * solved)
    return (solved[None], residual[None])


def solution(mesh):
    layers = mesh.shape["coord"] // 2
    plan = line_plan if layers == 4 else column_plan
    return jax.shard_map(
        plan,
        mesh=mesh,
        in_specs=(
            P("ka", "coord", None, None),
            P("coord", None, None),
            P("coord", None),
            P(),
            P(),
            P(),
            P(),
            P(),
            P(),
            P(),
            P(),
            P(),
            P(),
        ),
        out_specs=(P("ka", "coord", None, None), P("ka", "coord", None, None)),
        check_vma=False,
    )
```

```python
import functools

import jax
import jax.numpy as jnp
from jax import lax
from jax.experimental import pallas as pl
from jax.experimental.pallas import tpu as pltpu
from jax.sharding import PartitionSpec as P

highest = lax.Precision.HIGHEST
high = lax.Precision.HIGH
shift_energy = 2.5
damping = 0.5
vmem_limit = 56 * 1024 * 1024


def halves(value):
    leading = lax.reduce_precision(value, 8, 7)
    return leading.astype(jnp.bfloat16), (value - leading).astype(jnp.bfloat16)


def parts(value):
    leading = value.astype(jnp.bfloat16)
    return leading, (value - leading.astype(jnp.float32)).astype(jnp.bfloat16)


def product(left, right, dims=(((1,), (0,)), ((), ()))):
    dot = functools.partial(lax.dot_general, dimension_numbers=dims, preferred_element_type=jnp.float32)
    return dot(left[0], right[0]) + (dot(left[0], right[1]) + dot(left[1], right[0]))


def whole(array):
    return pl.BlockSpec(array.shape, lambda *_: (0,) * array.ndim)


def call(kernel, grid, in_specs, out_specs, out_shape, aliases={}):
    return pl.pallas_call(
        kernel,
        grid=grid,
        in_specs=in_specs,
        out_specs=out_specs,
        out_shape=out_shape,
        input_output_aliases=aliases,
        compiler_params=pltpu.CompilerParams(vmem_limit_bytes=vmem_limit),
    )


def f32(*shape):
    return jax.ShapeDtypeStruct(shape, jnp.float32)


def third_forward(source, weights):
    rows, columns, depth = source.shape
    step = 8
    width = weights[0].shape[0]

    def kernel(source_ref, first_ref, rest_ref, out_ref):
        weight = (first_ref[...], rest_ref[...])
        for row in range(step):
            out_ref[:, row, :] = product(weight, parts(source_ref[row]), (((1,), (1,)), ((), ())))

    return call(
        kernel,
        (rows // step,),
        [pl.BlockSpec((step, columns, depth), lambda g: (g, 0, 0)), whole(weights[0]), whole(weights[1])],
        pl.BlockSpec((width, step, columns), lambda g: (0, g, 0)),
        f32(width, rows, columns),
    )(source, *weights)


def front(value, weights, start, width, own=None, far_rows=None, layers=None, returned=None):
    _, rows, depth = value.shape
    half = weights[0].shape[1] // 2
    widths = [width or None] + [group[0].shape[0] for group in (far_rows, layers, returned) if group]
    grid = max(min(w for w in widths if w) // 4, 1)
    operands, in_specs, out_specs, out_shape = [], [], [], []

    def rows_of(array, index, tall=rows):
        deep = array.shape[0] // grid
        operands.append(array)
        in_specs.append(pl.BlockSpec((deep, tall, half), lambda g: (g, index, 0)))

    def result(deep, tall):
        out_specs.append(pl.BlockSpec((deep // grid, tall, half), lambda g: (g, 0, 0)))
        out_shape.append(f32(deep, tall, half))

    merged = bool(width and returned and returned[0].shape[0] == width)
    if width:
        deep = width // grid
        operands.append(value)
        in_specs.append(pl.BlockSpec((deep, rows, depth), lambda g: (start // deep + g, 0, 0)))
        for weight in weights:
            operands.append(weight)
            in_specs.append(whole(weight))
        result(width, rows)
        result(width, 3 * rows if merged else rows)
    if own is not None:
        rows_of(own, 0)
        rows_of(*far_rows)
        result(own.shape[0], 2 * rows)
    if layers:
        for array in layers:
            rows_of(array, 0, 2 * rows)
        result(layers[0].shape[0], 4 * rows)
    if returned:
        for array in returned:
            rows_of(array, 1, 2 * rows)
        if not merged:
            result(returned[0].shape[0], 2 * rows)

    def kernel(*refs):
        ins, outs = list(refs[: len(operands)]), list(refs[len(operands) :])
        away = None
        if width:
            value_ref, first_ref, rest_ref = ins[:3]
            del ins[:3]
            block = parts(value_ref[...].reshape(deep * rows, depth))
            out = product(block, (first_ref[...], rest_ref[...]))
            outs.pop(0)[...] = out[:, :half].reshape(deep, rows, half)
            away = outs.pop(0)
            away[:, :rows] = out[:, half:].reshape(deep, rows, half)
        if own is not None:
            both = outs.pop(0)
            both[:, :rows] = ins.pop(0)[...]
            both[:, rows:] = ins.pop(0)[...]
        if layers:
            across = outs.pop(0)
            across[:, : 2 * rows] = ins.pop(0)[...]
            across[:, 2 * rows :] = ins.pop(0)[...]
        if returned:
            total = ins[0][...] + ins[1][...]
            if merged:
                away[:, rows:] = total
            else:
                outs.pop(0)[...] = total

    got = list(call(kernel, (grid,), in_specs, out_specs, out_shape)(*operands))
    here = away = both = across = back = None
    if width:
        here, away = got.pop(0), got.pop(0)
    if own is not None:
        both = got.pop(0)
    if layers:
        across = got.pop(0)
    if returned and not merged:
        back = got.pop(0)
    return here, away, both, across, back, merged


def centre(blocks, inward, outward, first, second, third, start):
    width, rows, columns = blocks[0].shape
    rows //= 2
    step = min(width, 4)

    def kernel(third_ref, *refs):
        block_refs = refs[: len(blocks)]
        in_first, in_rest, out_first, out_rest, first_ref, second_ref, near_ref, far_ref = refs[len(blocks) :]
        for layer in range(step):
            value = jnp.concatenate([ref[layer] for ref in block_refs], axis=0)
            coeff = product((in_first[...], in_rest[...]), parts(value))
            angle = third_ref[start + pl.program_id(0) * step + layer]
            level = first_ref[...] + second_ref[...] + angle - shift_energy
            coeff = coeff * (level / (level * level + damping * damping))
            back = product((out_first[...], out_rest[...]), parts(coeff))
            near_ref[layer] = back[: 2 * rows]
            far_ref[layer] = back[2 * rows :]

    spec = pl.BlockSpec((step, 2 * rows, columns), lambda g: (g, 0, 0))
    small = (*inward, *outward, first, second)
    return call(
        kernel,
        (width // step,),
        [pl.BlockSpec(memory_space=pltpu.SMEM)] + [spec] * len(blocks) + [whole(a) for a in small],
        [spec, spec],
        [f32(width, 2 * rows, columns)] * 2,
    )(third, *blocks, *small)


def second_back(mine, other, full, weights, kinetic_weights, start, arrived=None, arrived_start=0):
    width, quad, half = mine[0].shape
    rows = quad // 4
    columns = weights[0].shape[1]
    step = min(width, 4)
    grid = width // step
    small = (*weights, *kinetic_weights)
    other, place = other
    extra = list(arrived or [])
    extra_deep = extra[0].shape[0] // grid if extra else 0

    def kernel(near_ref, returned_ref, first_other, second_other, first_ref, rest_ref, kin_first, kin_rest, *refs):
        extra_refs, outs = refs[: len(extra)], refs[len(extra) + 2 * bool(extra) + 2 :]
        total = near_ref[...] + returned_ref[...]
        block = [
            parts(
                jnp.concatenate(
                    [
                        total[:, term * rows : (term + 1) * rows, :].reshape(step * rows, half),
                        ref[...].reshape(step * rows, half),
                    ],
                    axis=1,
                )
            )
            for term, ref in enumerate((first_other, second_other))
        ]
        weight = (first_ref[...], rest_ref[...])
        solved = product(block[0], weight).reshape(step, rows, columns)
        outs[0][...] = solved
        outs[1][...] = solved
        kinetic = product(block[1], weight) + product(block[0], (kin_first[...], kin_rest[...]))
        outs[2][...] = kinetic.reshape(step, rows, columns)
        for ref, out in zip(extra_refs, outs[3:]):
            out[...] = ref[...]

    def layers(deep, first):
        return pl.BlockSpec((deep, rows, columns), lambda g: (first // deep + g, 0, 0))

    def rows_at(index, tall):
        return pl.BlockSpec((step, tall, half), lambda g: (g, index, 0))

    kept = list(full if extra else full[:2])
    operands = [*mine, other, other, *small, *extra, *kept]
    first_kept = len(operands) - len(kept)
    got = call(
        kernel,
        (grid,),
        [rows_at(0, 2 * rows)] * 2
        + [rows_at(place, rows), rows_at(place + 1, rows)]
        + [whole(a) for a in small]
        + [layers(extra_deep, 0)] * len(extra)
        + [pl.BlockSpec(memory_space=pl.ANY)] * len(kept),
        [layers(step, 0)] + [layers(step, start)] * 2 + ([layers(extra_deep, arrived_start)] * 2 if extra else []),
        [f32(width, rows, columns)] + [f32(*a.shape) for a in kept],
        {first_kept + n: 1 + n for n in range(len(kept))},
    )(*operands)
    return got[0], tuple(got[1:]) + tuple(full[len(kept) :])


def third_back(solved, kinetic, even, odd, source, potential, rotation, weights, coupling_weights, square):
    depth, rows, columns = solved.shape
    width = source.shape[2]
    step = 8

    def kernel(square_ref, solved_ref, kinetic_ref, even_ref, odd_ref, source_ref, potential_ref, rotation_ref, *refs):
        first_ref, rest_ref, mix_first, mix_rest, out_ref, residual_ref = refs
        weight = (first_ref[...], rest_ref[...])
        mix = (mix_first[...], mix_rest[...])
        for row in range(step):
            both = product(
                weight, parts(jnp.concatenate([solved_ref[:, row, :], kinetic_ref[:, row, :]], axis=0))
            )
            coupled = product(mix, parts(jnp.concatenate([even_ref[:, row, :], odd_ref[:, row, :]], axis=0)))
            upper, lower = both[:width], both[width:]
            factor = rotation_ref[row : row + 1, :]
            lower = lower + factor * (coupled + square_ref[0, 0] * upper) - shift_energy * upper
            upper, lower = upper.T, lower.T
            out_ref[row] = upper
            residual_ref[row] = source_ref[row] - (lower + potential_ref[row] * upper)

    layer = pl.BlockSpec((depth, step, columns // 2), lambda g, h: (0, g, h))
    slab = pl.BlockSpec((step, columns // 2, width), lambda g, h: (g, h, 0))
    small = (*weights, *coupling_weights)
    return call(
        kernel,
        (rows // step, 2),
        [pl.BlockSpec(memory_space=pltpu.SMEM)]
        + [layer] * 4
        + [slab] * 2
        + [pl.BlockSpec((step, columns // 2), lambda g, h: (g, h))]
        + [whole(a) for a in small],
        [slab, slab],
        [f32(*source.shape)] * 2,
    )(square, solved, kinetic, even, odd, source, potential, rotation, *small)


def unwritten(shape, count):
    def kernel(*refs):
        pass

    anywhere = pl.BlockSpec(memory_space=pl.ANY)
    return pl.pallas_call(kernel, out_specs=[anywhere] * count, out_shape=[f32(*shape)] * count)()


def chunk_widths(total):
    unit = total // 16
    small = unit // 2
    return [small] * 2 + [unit] * 14 + [small] * 2


def line_plan(
    states,
    potential,
    rotation_factor,
    basis_first,
    basis_second,
    basis_third,
    levels_first,
    levels_second,
    levels_third,
    kinetic_first,
    kinetic_second,
    kinetic_third,
    coriolis_matrix,
):
    source = states[0]
    count = lax.axis_size("coord")
    blocks = lax.axis_size("ka")
    coord = lax.axis_index("coord")
    kindex = lax.axis_index("ka")
    layer, side = coord // 2, coord % 2
    layers = count // 2
    rows, second_size, third_size = source.shape
    first_size = basis_first.shape[0]
    half = second_size // 2
    dot = functools.partial(jnp.dot, precision=highest)

    def place(z, y):
        return 2 * z + y

    sides = range(2)
    inner = (layers // 2 - 1, layers // 2)
    to_inner = [(place(z ^ 1, y), place(z, y)) for z in inner for y in sides]
    to_outer = [(b, a) for a, b in to_inner]
    across_middle = [(place(z, y), place(layers - 1 - z, y)) for z in inner for y in sides]
    facing_side = [(place(z, y), place(z, 1 - y)) for z in range(layers) for y in sides]
    even_pairs = [pair for k in range(0, blocks - 1, 2) for pair in ((k, k + 1), (k + 1, k))]
    odd_pairs = [pair for k in range(1, blocks - 1, 2) for pair in ((k, k + 1), (k + 1, k))]

    def mine_first(matrix, axis):
        return jnp.roll(matrix, -side * half, axis)

    weights_third = halves(basis_third.T)
    layered = third_forward(source, weights_third)
    basis_mine = mine_first(basis_second, 1)
    weights_second = halves(basis_mine)

    def prepare(gate):
        tied = lax.optimization_barrier((gate, basis_first, basis_mine, basis_third, kinetic_first))
        gate, first, second, third, kin_first = tied
        kinetic_basis = dot(kin_first, first)
        is_inner = jnp.logical_and(layer >= inner[0], layer <= inner[1]).astype(jnp.float32)

        def block(matrix, z, y):
            return lax.dynamic_slice_in_dim(matrix, (2 * z + y) * rows, rows)

        pair_layer = layer ^ 1
        facing = layers - 1 - layer
        both_sides = (side, 1 - side)
        order = [(z, y) for z in (layer, pair_layer, facing, facing ^ 1) for y in both_sides]
        inward = jnp.concatenate([block(first, z, y) for z, y in order], axis=0).T
        near = jnp.concatenate([block(m, layer, y) for y in both_sides for m in (first, kinetic_basis)], axis=0)
        far = jnp.concatenate([block(m, pair_layer, y) for y in both_sides for m in (first, kinetic_basis)], axis=0)
        outward = jnp.concatenate([near * is_inner, far], axis=0)
        turned = second.T
        kinetic_turned = dot(kinetic_second, second).T
        kval = kindex.astype(jnp.float32)
        square_top = (blocks - 1) * blocks
        coupled_up = jnp.sqrt(square_top - kval * (kval + 1.0))
        coupled_down = jnp.sqrt(square_top - (kval - 1.0) * kval)
        up = coupled_up * dot(coriolis_matrix, third)
        down = coupled_down * dot(coriolis_matrix.T, third)
        is_even = kindex % 2 == 0
        mix = jnp.concatenate([jnp.where(is_even, up, down), jnp.where(is_even, down, up)], axis=1)
        both = jnp.concatenate(
            [
                jnp.concatenate([third, jnp.zeros_like(third)], axis=1),
                jnp.concatenate([dot(kinetic_third, third), third], axis=1),
            ],
            axis=0,
        )
        return gate, dict(
            inward=halves(inward),
            outward=halves(outward),
            turned=halves(turned),
            kinetic_turned=halves(kinetic_turned),
            both=halves(both),
            mix=halves(mix),
            square=(kval * kval).reshape(1, 1),
            first=levels_first[:, None],
            second=lax.dynamic_slice_in_dim(levels_second, side * half, half)[None, :],
        )

    widths = chunk_widths(third_size)
    starts = [sum(widths[:q]) for q in range(len(widths))]
    total = len(widths)
    full = unwritten((third_size, rows, second_size), 4)

    ready, place_back, table = {}, {}, None
    for step in range(total + 12):
        made = {}
        chunk = [step - stage for stage in range(13)]
        live = [0 <= q < total for q in chunk]

        def send(name, key, axis, pairs):
            made[key] = lax.ppermute(ready[name], axis, pairs)

        def turn(q):
            made["near", q], made["far", q] = centre(
                (ready["layers", q], ready["facing", q]),
                table["inward"],
                table["outward"],
                table["first"],
                table["second"],
                levels_third,
                starts[q],
            )

        if chunk[6] == total - 1:
            turn(chunk[6])
            names = [key for key in ready if key != ("far", chunk[7])]
            made, held = lax.optimization_barrier((made, [ready[key] for key in names]))
            ready.update(zip(names, held))
        if live[5]:
            send(("layers", chunk[5]), ("facing", chunk[5]), "coord", across_middle)
        if live[7] and ("returned", chunk[7]) not in ready:
            send(("far", chunk[7]), ("returned", chunk[7]), "coord", to_outer)
        if live[3]:
            send(("own", chunk[3]), ("outer", chunk[3]), "coord", to_inner)
        if live[1]:
            send(("away", chunk[1]), ("rows in", chunk[1]), "coord", facing_side)
        if live[9] and ("rows back", chunk[9]) not in ready:
            q = chunk[9]
            if ("back", q) in ready:
                send(("back", q), ("rows back", q), "coord", facing_side)
                place_back[q] = 0
            else:
                made["rows back", q] = made["rows in", chunk[1]]
                place_back[q] = 1
        if live[11]:
            send(("solved", chunk[11]), ("even", chunk[11]), "ka", even_pairs)
            send(("solved", chunk[11]), ("odd", chunk[11]), "ka", odd_pairs)

        if any(live[stage] for stage in (0, 2, 4, 8)):
            here, away, both, layers_rows, back, merged = front(
                layered,
                weights_second,
                starts[chunk[0]] if live[0] else 0,
                widths[chunk[0]] if live[0] else 0,
                ready["here", chunk[2]] if live[2] else None,
                (ready["rows in", chunk[2]], 0) if live[2] else None,
                (ready["own", chunk[4]], ready["outer", chunk[4]]) if live[4] else None,
                (ready["near", chunk[8]], ready["returned", chunk[8]]) if live[8] else None,
            )
            if live[0]:
                made["here", chunk[0]], made["away", chunk[0]] = here, away
            if live[2]:
                made["own", chunk[2]] = both
            if live[4]:
                made["layers", chunk[4]] = layers_rows
            if live[8] and not merged:
                made["back", chunk[8]] = back
        if step == 1:
            ready["away", 0], table = prepare(ready["away", 0])
        if live[10]:
            q, late = chunk[10], chunk[12]
            made["solved", q], full = second_back(
                (ready["near", q], ready["returned", q]),
                (ready["rows back", q], place_back[q]),
                full,
                table["turned"],
                table["kinetic_turned"],
                starts[q],
                [ready["even", late], ready["odd", late]] if live[12] else None,
                starts[late] if live[12] else 0,
            )
        elif live[12]:
            q, full = chunk[12], list(full)
            for slot, name in ((2, "even"), (3, "odd")):
                full[slot] = lax.dynamic_update_slice(full[slot], ready[name, q], (starts[q], 0, 0))
            full = tuple(full)
        if live[6] and chunk[6] < total - 1:
            turn(chunk[6])
        if chunk[6] == total - 1:
            made["returned", chunk[6]] = lax.ppermute(made["far", chunk[6]], "coord", to_outer)
            if ("back", chunk[8]) in made:
                made["rows back", chunk[8]] = lax.ppermute(made["back", chunk[8]], "coord", facing_side)
                place_back[chunk[8]] = 0
        last_use = {
            "here": 2,
            "away": 1,
            "rows in": 2,
            "own": 4,
            "outer": 4,
            "layers": 6,
            "facing": 6,
            "near": 10,
            "far": 7,
            "returned": 10,
            "back": 9,
            "rows back": 10,
            "solved": 11,
            "even": 12,
            "odd": 12,
        }
        ready = {key: array for key, array in ready.items() if step - key[1] < last_use[key[0]]}
        ready.update(made)
        if chunk[6] < total:
            (layered, full), ready = lax.optimization_barrier(((layered, full), ready))
    full = list(full)
    for q in range(total):
        for place_of, name in ((2, "even"), (3, "odd")):
            if (name, q) in ready:
                full[place_of] = lax.dynamic_update_slice(full[place_of], ready.pop((name, q)), (starts[q], 0, 0))
    solved_full, kinetic_full, even_full, odd_full = full

    solved, residual = third_back(
        solved_full,
        kinetic_full,
        even_full,
        odd_full,
        source,
        potential,
        rotation_factor,
        table["both"],
        table["mix"],
        table["square"],
    )
    return (solved[None], residual[None])


def from_behind(value, axis, steps):
    count = lax.axis_size(axis)
    leading, last = (max(0, -steps), min(count, count - steps))
    return lax.ppermute(value, axis, [(source, source + steps) for source in range(leading, last)])


def finish_slab(back, basis_second, basis_third):
    back = jnp.einsum("jb,ibc->ijc", basis_second, back, precision=high)
    return jnp.einsum("kc,ijc->ijk", basis_third, back, precision=high)


def column_plan(
    states,
    potential,
    rotation_factor,
    basis_first,
    basis_second,
    basis_third,
    levels_first,
    levels_second,
    levels_third,
    kinetic_first,
    kinetic_second,
    kinetic_third,
    coriolis_matrix,
):
    source = states[0]
    coeff = jnp.einsum("ijk,kc->ijc", source, basis_third, precision=high)
    coeff = jnp.einsum("ijc,jb->ibc", coeff, basis_second, precision=high)
    columns = lax.all_to_all(coeff, "coord", split_axis=1, concat_axis=0, tiled=True)
    width = columns.shape[1]
    start = lax.axis_index("coord") * width
    local_second = lax.dynamic_slice_in_dim(levels_second, start, width)
    level = (
        levels_first[:, None, None]
        + local_second[None, :, None]
        + levels_third[None, None, :]
        - shift_energy
    )
    filt = level / (level * level + damping * damping)
    columns = jnp.einsum("ibc,ia->abc", columns, basis_first, precision=high)
    columns = columns * filt
    back = jnp.einsum("ia,abc->ibc", basis_first, columns, precision=high)
    kinetic_back = jnp.einsum("im,mbc->ibc", kinetic_first, back, precision=high)
    back_rows, kinetic_rows = (
        lax.all_to_all(back, "coord", split_axis=0, concat_axis=1, tiled=True),
        lax.all_to_all(kinetic_back, "coord", split_axis=0, concat_axis=1, tiled=True),
    )
    solved = finish_slab(back_rows, basis_second, basis_third)
    kinetic = finish_slab(kinetic_rows, basis_second, basis_third)
    above = from_behind(solved, "ka", -1)
    below = from_behind(solved, "ka", 1)
    kinetic = kinetic + jnp.einsum("jm,imk->ijk", kinetic_second, solved, precision=high)
    kinetic = kinetic + jnp.einsum("km,ijm->ijk", kinetic_third, solved, precision=high)
    kval = lax.axis_index("ka").astype(jnp.float32)
    blocks = lax.axis_size("ka")
    square_top = (blocks - 1) * blocks
    coupled_up = jnp.sqrt(square_top - kval * (kval + 1.0))
    coupled_down = jnp.sqrt(square_top - (kval - 1.0) * kval)
    factor = rotation_factor[:, :, None]
    from_upper = jnp.einsum("km,ijm->ijk", coriolis_matrix, above, precision=high)
    from_lower = jnp.einsum("mk,ijm->ijk", coriolis_matrix, below, precision=high)
    coupling = factor * (coupled_up * from_upper + coupled_down * from_lower)
    applied = kinetic + (potential + kval * kval * factor) * solved + coupling
    residual = source - (applied - shift_energy * solved)
    return (solved[None], residual[None])


def solution(mesh):
    layers = mesh.shape["coord"] // 2
    plan = line_plan if layers == 4 else column_plan
    return jax.shard_map(
        plan,
        mesh=mesh,
        in_specs=(
            P("ka", "coord", None, None),
            P("coord", None, None),
            P("coord", None),
            P(),
            P(),
            P(),
            P(),
            P(),
            P(),
            P(),
            P(),
            P(),
            P(),
        ),
        out_specs=(P("ka", "coord", None, None), P("ka", "coord", None, None)),
        check_vma=False,
    )
```

```python
import functools

import jax
import jax.numpy as jnp
from jax import lax
from jax.experimental import pallas as pl
from jax.experimental.pallas import tpu as pltpu
from jax.sharding import PartitionSpec as P

highest = lax.Precision.HIGHEST
high = lax.Precision.HIGH
shift_energy = 2.5
damping = 0.5
vmem_limit = 56 * 1024 * 1024


def halves(value):
    leading = lax.reduce_precision(value, 8, 7)
    return leading.astype(jnp.bfloat16), (value - leading).astype(jnp.bfloat16)


def parts(value):
    leading = value.astype(jnp.bfloat16)
    return leading, (value - leading.astype(jnp.float32)).astype(jnp.bfloat16)


def product(left, right, dims=(((1,), (0,)), ((), ()))):
    dot = functools.partial(lax.dot_general, dimension_numbers=dims, preferred_element_type=jnp.float32)
    return dot(left[0], right[0]) + (dot(left[0], right[1]) + dot(left[1], right[0]))


def whole(array):
    return pl.BlockSpec(array.shape, lambda *_: (0,) * array.ndim)


def call(kernel, grid, in_specs, out_specs, out_shape, aliases={}):
    return pl.pallas_call(
        kernel,
        grid=grid,
        in_specs=in_specs,
        out_specs=out_specs,
        out_shape=out_shape,
        input_output_aliases=aliases,
        compiler_params=pltpu.CompilerParams(vmem_limit_bytes=vmem_limit),
    )


def f32(*shape):
    return jax.ShapeDtypeStruct(shape, jnp.float32)


def third_forward(source, weights):
    rows, columns, depth = source.shape
    step = 8
    width = weights[0].shape[0]

    def kernel(source_ref, first_ref, rest_ref, out_ref):
        weight = (first_ref[...], rest_ref[...])
        for row in range(step):
            out_ref[:, row, :] = product(weight, parts(source_ref[row]), (((1,), (1,)), ((), ())))

    return call(
        kernel,
        (rows // step,),
        [pl.BlockSpec((step, columns, depth), lambda g: (g, 0, 0)), whole(weights[0]), whole(weights[1])],
        pl.BlockSpec((width, step, columns), lambda g: (0, g, 0)),
        f32(width, rows, columns),
    )(source, *weights)


def front(value, weights, start, width, own=None, far_rows=None, layers=None, returned=None):
    _, rows, depth = value.shape
    half = weights[0].shape[1] // 2
    widths = [width or None] + [group[0].shape[0] for group in (far_rows, layers, returned) if group]
    grid = max(min(w for w in widths if w) // 4, 1)
    operands, in_specs, out_specs, out_shape = [], [], [], []

    def rows_of(array, index, tall=rows):
        deep = array.shape[0] // grid
        operands.append(array)
        in_specs.append(pl.BlockSpec((deep, tall, half), lambda g: (g, index, 0)))

    def result(deep, tall):
        out_specs.append(pl.BlockSpec((deep // grid, tall, half), lambda g: (g, 0, 0)))
        out_shape.append(f32(deep, tall, half))

    merged = bool(width and returned and returned[0].shape[0] == width)
    if width:
        deep = width // grid
        operands.append(value)
        in_specs.append(pl.BlockSpec((deep, rows, depth), lambda g: (start // deep + g, 0, 0)))
        for weight in weights:
            operands.append(weight)
            in_specs.append(whole(weight))
        result(width, rows)
        result(width, 3 * rows if merged else rows)
    if own is not None:
        rows_of(own, 0)
        rows_of(*far_rows)
        result(own.shape[0], 2 * rows)
    if layers:
        for array in layers:
            rows_of(array, 0, 2 * rows)
        result(layers[0].shape[0], 4 * rows)
    if returned:
        for array in returned:
            rows_of(array, 1, 2 * rows)
        if not merged:
            result(returned[0].shape[0], 2 * rows)

    def kernel(*refs):
        ins, outs = list(refs[: len(operands)]), list(refs[len(operands) :])
        away = None
        if width:
            value_ref, first_ref, rest_ref = ins[:3]
            del ins[:3]
            block = parts(value_ref[...].reshape(deep * rows, depth))
            out = product(block, (first_ref[...], rest_ref[...]))
            outs.pop(0)[...] = out[:, :half].reshape(deep, rows, half)
            away = outs.pop(0)
            away[:, :rows] = out[:, half:].reshape(deep, rows, half)
        if own is not None:
            both = outs.pop(0)
            both[:, :rows] = ins.pop(0)[...]
            both[:, rows:] = ins.pop(0)[...]
        if layers:
            across = outs.pop(0)
            across[:, : 2 * rows] = ins.pop(0)[...]
            across[:, 2 * rows :] = ins.pop(0)[...]
        if returned:
            total = ins[0][...] + ins[1][...]
            if merged:
                away[:, rows:] = total
            else:
                outs.pop(0)[...] = total

    got = list(call(kernel, (grid,), in_specs, out_specs, out_shape)(*operands))
    here = away = both = across = back = None
    if width:
        here, away = got.pop(0), got.pop(0)
    if own is not None:
        both = got.pop(0)
    if layers:
        across = got.pop(0)
    if returned and not merged:
        back = got.pop(0)
    return here, away, both, across, back, merged


def centre(blocks, inward, outward, first, second, third, start):
    width, rows, columns = blocks[0].shape
    rows //= 2
    step = min(width, 4)

    def kernel(third_ref, *refs):
        block_refs = refs[: len(blocks)]
        in_first, in_rest, out_first, out_rest, first_ref, second_ref, near_ref, far_ref = refs[len(blocks) :]
        for layer in range(step):
            value = jnp.concatenate([ref[layer] for ref in block_refs], axis=0)
            coeff = product((in_first[...], in_rest[...]), parts(value))
            angle = third_ref[start + pl.program_id(0) * step + layer]
            level = first_ref[...] + second_ref[...] + angle - shift_energy
            coeff = coeff * (level / (level * level + damping * damping))
            back = product((out_first[...], out_rest[...]), parts(coeff))
            near_ref[layer] = back[: 2 * rows]
            far_ref[layer] = back[2 * rows :]

    spec = pl.BlockSpec((step, 2 * rows, columns), lambda g: (g, 0, 0))
    small = (*inward, *outward, first, second)
    return call(
        kernel,
        (width // step,),
        [pl.BlockSpec(memory_space=pltpu.SMEM)] + [spec] * len(blocks) + [whole(a) for a in small],
        [spec, spec],
        [f32(width, 2 * rows, columns)] * 2,
    )(third, *blocks, *small)


def second_back(mine, other, full, weights, kinetic_weights, start, arrived=None, arrived_start=0):
    width, quad, half = mine[0].shape
    rows = quad // 4
    columns = weights[0].shape[1]
    step = min(width, 4)
    grid = width // step
    small = (*weights, *kinetic_weights)
    other, place = other
    extra = list(arrived or [])
    extra_deep = extra[0].shape[0] // grid if extra else 0

    def kernel(near_ref, returned_ref, first_other, second_other, first_ref, rest_ref, kin_first, kin_rest, *refs):
        extra_refs, outs = refs[: len(extra)], refs[len(extra) + 2 * bool(extra) + 2 :]
        total = near_ref[...] + returned_ref[...]
        block = [
            parts(
                jnp.concatenate(
                    [
                        total[:, term * rows : (term + 1) * rows, :].reshape(step * rows, half),
                        ref[...].reshape(step * rows, half),
                    ],
                    axis=1,
                )
            )
            for term, ref in enumerate((first_other, second_other))
        ]
        weight = (first_ref[...], rest_ref[...])
        solved = product(block[0], weight).reshape(step, rows, columns)
        outs[0][...] = solved
        outs[1][...] = solved
        kinetic = product(block[1], weight) + product(block[0], (kin_first[...], kin_rest[...]))
        outs[2][...] = kinetic.reshape(step, rows, columns)
        for ref, out in zip(extra_refs, outs[3:]):
            out[...] = ref[...]

    def layers(deep, first):
        return pl.BlockSpec((deep, rows, columns), lambda g: (first // deep + g, 0, 0))

    def rows_at(index, tall):
        return pl.BlockSpec((step, tall, half), lambda g: (g, index, 0))

    kept = list(full if extra else full[:2])
    operands = [*mine, other, other, *small, *extra, *kept]
    first_kept = len(operands) - len(kept)
    got = call(
        kernel,
        (grid,),
        [rows_at(0, 2 * rows)] * 2
        + [rows_at(place, rows), rows_at(place + 1, rows)]
        + [whole(a) for a in small]
        + [layers(extra_deep, 0)] * len(extra)
        + [pl.BlockSpec(memory_space=pl.ANY)] * len(kept),
        [layers(step, 0)] + [layers(step, start)] * 2 + ([layers(extra_deep, arrived_start)] * 2 if extra else []),
        [f32(width, rows, columns)] + [f32(*a.shape) for a in kept],
        {first_kept + n: 1 + n for n in range(len(kept))},
    )(*operands)
    return got[0], tuple(got[1:]) + tuple(full[len(kept) :])


def third_back(solved, kinetic, even, odd, source, potential, rotation, weights, coupling_weights, square):
    depth, rows, columns = solved.shape
    width = source.shape[2]
    step = 8

    def kernel(square_ref, solved_ref, kinetic_ref, even_ref, odd_ref, source_ref, potential_ref, rotation_ref, *refs):
        first_ref, rest_ref, mix_first, mix_rest, out_ref, residual_ref = refs
        weight = (first_ref[...], rest_ref[...])
        mix = (mix_first[...], mix_rest[...])
        for row in range(step):
            both = product(
                weight, parts(jnp.concatenate([solved_ref[:, row, :], kinetic_ref[:, row, :]], axis=0))
            )
            coupled = product(mix, parts(jnp.concatenate([even_ref[:, row, :], odd_ref[:, row, :]], axis=0)))
            upper, lower = both[:width], both[width:]
            factor = rotation_ref[row : row + 1, :]
            lower = lower + factor * (coupled + square_ref[0, 0] * upper) - shift_energy * upper
            upper, lower = upper.T, lower.T
            out_ref[row] = upper
            residual_ref[row] = source_ref[row] - (lower + potential_ref[row] * upper)

    layer = pl.BlockSpec((depth, step, columns // 2), lambda g, h: (0, g, h))
    slab = pl.BlockSpec((step, columns // 2, width), lambda g, h: (g, h, 0))
    small = (*weights, *coupling_weights)
    return call(
        kernel,
        (rows // step, 2),
        [pl.BlockSpec(memory_space=pltpu.SMEM)]
        + [layer] * 4
        + [slab] * 2
        + [pl.BlockSpec((step, columns // 2), lambda g, h: (g, h))]
        + [whole(a) for a in small],
        [slab, slab],
        [f32(*source.shape)] * 2,
    )(square, solved, kinetic, even, odd, source, potential, rotation, *small)


def unwritten(shape, count):
    def kernel(*refs):
        pass

    anywhere = pl.BlockSpec(memory_space=pl.ANY)
    return pl.pallas_call(kernel, out_specs=[anywhere] * count, out_shape=[f32(*shape)] * count)()


def chunk_widths(total):
    unit = total // 16
    small = unit // 2
    return [small] * 2 + [unit] * 14 + [small] * 2


def line_plan(
    states,
    potential,
    rotation_factor,
    basis_first,
    basis_second,
    basis_third,
    levels_first,
    levels_second,
    levels_third,
    kinetic_first,
    kinetic_second,
    kinetic_third,
    coriolis_matrix,
):
    source = states[0]
    count = lax.axis_size("coord")
    blocks = lax.axis_size("ka")
    coord = lax.axis_index("coord")
    kindex = lax.axis_index("ka")
    layer, side = coord // 2, coord % 2
    layers = count // 2
    rows, second_size, third_size = source.shape
    first_size = basis_first.shape[0]
    half = second_size // 2
    dot = functools.partial(jnp.dot, precision=highest)

    def place(z, y):
        return 2 * z + y

    sides = range(2)
    inner = (layers // 2 - 1, layers // 2)
    to_inner = [(place(z ^ 1, y), place(z, y)) for z in inner for y in sides]
    to_outer = [(b, a) for a, b in to_inner]
    across_middle = [(place(z, y), place(layers - 1 - z, y)) for z in inner for y in sides]
    facing_side = [(place(z, y), place(z, 1 - y)) for z in range(layers) for y in sides]
    even_pairs = [pair for k in range(0, blocks - 1, 2) for pair in ((k, k + 1), (k + 1, k))]
    odd_pairs = [pair for k in range(1, blocks - 1, 2) for pair in ((k, k + 1), (k + 1, k))]

    def mine_first(matrix, axis):
        return jnp.roll(matrix, -side * half, axis)

    weights_third = halves(basis_third.T)
    layered = third_forward(source, weights_third)
    basis_mine = mine_first(basis_second, 1)
    weights_second = halves(basis_mine)

    def prepare(gate):
        tied = lax.optimization_barrier((gate, basis_first, basis_mine, basis_third, kinetic_first))
        gate, first, second, third, kin_first = tied
        kinetic_basis = dot(kin_first, first)
        is_inner = jnp.logical_and(layer >= inner[0], layer <= inner[1]).astype(jnp.float32)

        def block(matrix, z, y):
            return lax.dynamic_slice_in_dim(matrix, (2 * z + y) * rows, rows)

        pair_layer = layer ^ 1
        facing = layers - 1 - layer
        both_sides = (side, 1 - side)
        order = [(z, y) for z in (layer, pair_layer, facing, facing ^ 1) for y in both_sides]
        inward = jnp.concatenate([block(first, z, y) for z, y in order], axis=0).T
        near = jnp.concatenate([block(m, layer, y) for y in both_sides for m in (first, kinetic_basis)], axis=0)
        far = jnp.concatenate([block(m, pair_layer, y) for y in both_sides for m in (first, kinetic_basis)], axis=0)
        outward = jnp.concatenate([near * is_inner, far], axis=0)
        turned = second.T
        kinetic_turned = dot(kinetic_second, second).T
        kval = kindex.astype(jnp.float32)
        square_top = (blocks - 1) * blocks
        coupled_up = jnp.sqrt(square_top - kval * (kval + 1.0))
        coupled_down = jnp.sqrt(square_top - (kval - 1.0) * kval)
        up = coupled_up * dot(coriolis_matrix, third)
        down = coupled_down * dot(coriolis_matrix.T, third)
        is_even = kindex % 2 == 0
        mix = jnp.concatenate([jnp.where(is_even, up, down), jnp.where(is_even, down, up)], axis=1)
        both = jnp.concatenate(
            [
                jnp.concatenate([third, jnp.zeros_like(third)], axis=1),
                jnp.concatenate([dot(kinetic_third, third), third], axis=1),
            ],
            axis=0,
        )
        return gate, dict(
            inward=halves(inward),
            outward=halves(outward),
            turned=halves(turned),
            kinetic_turned=halves(kinetic_turned),
            both=halves(both),
            mix=halves(mix),
            square=(kval * kval).reshape(1, 1),
            first=levels_first[:, None],
            second=lax.dynamic_slice_in_dim(levels_second, side * half, half)[None, :],
        )

    widths = chunk_widths(third_size)
    starts = [sum(widths[:q]) for q in range(len(widths))]
    total = len(widths)
    full = unwritten((third_size, rows, second_size), 4)

    ready, place_back, table = {}, {}, None
    for step in range(total + 12):
        made = {}
        chunk = [step - stage for stage in range(13)]
        live = [0 <= q < total for q in chunk]

        def send(name, key, axis, pairs):
            made[key] = lax.ppermute(ready[name], axis, pairs)

        def turn(q):
            made["near", q], made["far", q] = centre(
                (ready["layers", q], ready["facing", q]),
                table["inward"],
                table["outward"],
                table["first"],
                table["second"],
                levels_third,
                starts[q],
            )

        if chunk[6] == total - 1:
            turn(chunk[6])
            names = [key for key in ready if key[0] not in ("far", "solved", "back")]
            made, held = lax.optimization_barrier((made, [ready[key] for key in names]))
            ready.update(zip(names, held))
        if live[5]:
            send(("layers", chunk[5]), ("facing", chunk[5]), "coord", across_middle)
        if live[7] and ("returned", chunk[7]) not in ready:
            send(("far", chunk[7]), ("returned", chunk[7]), "coord", to_outer)
        if live[3]:
            send(("own", chunk[3]), ("outer", chunk[3]), "coord", to_inner)
        if live[1]:
            send(("away", chunk[1]), ("rows in", chunk[1]), "coord", facing_side)
        if live[9] and ("rows back", chunk[9]) not in ready:
            q = chunk[9]
            if ("back", q) in ready:
                send(("back", q), ("rows back", q), "coord", facing_side)
                place_back[q] = 0
            else:
                made["rows back", q] = made["rows in", chunk[1]]
                place_back[q] = 1
        if live[11]:
            send(("solved", chunk[11]), ("even", chunk[11]), "ka", even_pairs)
            send(("solved", chunk[11]), ("odd", chunk[11]), "ka", odd_pairs)

        if any(live[stage] for stage in (0, 2, 4, 8)):
            here, away, both, layers_rows, back, merged = front(
                layered,
                weights_second,
                starts[chunk[0]] if live[0] else 0,
                widths[chunk[0]] if live[0] else 0,
                ready["here", chunk[2]] if live[2] else None,
                (ready["rows in", chunk[2]], 0) if live[2] else None,
                (ready["own", chunk[4]], ready["outer", chunk[4]]) if live[4] else None,
                (ready["near", chunk[8]], ready["returned", chunk[8]]) if live[8] else None,
            )
            if live[0]:
                made["here", chunk[0]], made["away", chunk[0]] = here, away
            if live[2]:
                made["own", chunk[2]] = both
            if live[4]:
                made["layers", chunk[4]] = layers_rows
            if live[8] and not merged:
                made["back", chunk[8]] = back
        if step == 1:
            ready["away", 0], table = prepare(ready["away", 0])
        if live[10]:
            q, late = chunk[10], chunk[12]
            made["solved", q], full = second_back(
                (ready["near", q], ready["returned", q]),
                (ready["rows back", q], place_back[q]),
                full,
                table["turned"],
                table["kinetic_turned"],
                starts[q],
                [ready["even", late], ready["odd", late]] if live[12] else None,
                starts[late] if live[12] else 0,
            )
        elif live[12]:
            q, full = chunk[12], list(full)
            for slot, name in ((2, "even"), (3, "odd")):
                full[slot] = lax.dynamic_update_slice(full[slot], ready[name, q], (starts[q], 0, 0))
            full = tuple(full)
        if live[6] and chunk[6] < total - 1:
            turn(chunk[6])
        if chunk[6] == total - 1:
            made["returned", chunk[6]] = lax.ppermute(made["far", chunk[6]], "coord", to_outer)
            if ("back", chunk[8]) in made:
                made["rows back", chunk[8]] = lax.ppermute(made["back", chunk[8]], "coord", facing_side)
                place_back[chunk[8]] = 0
        last_use = {
            "here": 2,
            "away": 1,
            "rows in": 2,
            "own": 4,
            "outer": 4,
            "layers": 6,
            "facing": 6,
            "near": 10,
            "far": 7,
            "returned": 10,
            "back": 9,
            "rows back": 10,
            "solved": 11,
            "even": 12,
            "odd": 12,
        }
        ready = {key: array for key, array in ready.items() if step - key[1] < last_use[key[0]]}
        ready.update(made)
        if chunk[6] < total:
            (layered, full), ready = lax.optimization_barrier(((layered, full), ready))
    full = list(full)
    for q in range(total):
        for place_of, name in ((2, "even"), (3, "odd")):
            if (name, q) in ready:
                full[place_of] = lax.dynamic_update_slice(full[place_of], ready.pop((name, q)), (starts[q], 0, 0))
    solved_full, kinetic_full, even_full, odd_full = full

    solved, residual = third_back(
        solved_full,
        kinetic_full,
        even_full,
        odd_full,
        source,
        potential,
        rotation_factor,
        table["both"],
        table["mix"],
        table["square"],
    )
    return (solved[None], residual[None])


def from_behind(value, axis, steps):
    count = lax.axis_size(axis)
    leading, last = (max(0, -steps), min(count, count - steps))
    return lax.ppermute(value, axis, [(source, source + steps) for source in range(leading, last)])


def finish_slab(back, basis_second, basis_third):
    back = jnp.einsum("jb,ibc->ijc", basis_second, back, precision=high)
    return jnp.einsum("kc,ijc->ijk", basis_third, back, precision=high)


def column_plan(
    states,
    potential,
    rotation_factor,
    basis_first,
    basis_second,
    basis_third,
    levels_first,
    levels_second,
    levels_third,
    kinetic_first,
    kinetic_second,
    kinetic_third,
    coriolis_matrix,
):
    source = states[0]
    coeff = jnp.einsum("ijk,kc->ijc", source, basis_third, precision=high)
    coeff = jnp.einsum("ijc,jb->ibc", coeff, basis_second, precision=high)
    columns = lax.all_to_all(coeff, "coord", split_axis=1, concat_axis=0, tiled=True)
    width = columns.shape[1]
    start = lax.axis_index("coord") * width
    local_second = lax.dynamic_slice_in_dim(levels_second, start, width)
    level = (
        levels_first[:, None, None]
        + local_second[None, :, None]
        + levels_third[None, None, :]
        - shift_energy
    )
    filt = level / (level * level + damping * damping)
    columns = jnp.einsum("ibc,ia->abc", columns, basis_first, precision=high)
    columns = columns * filt
    back = jnp.einsum("ia,abc->ibc", basis_first, columns, precision=high)
    kinetic_back = jnp.einsum("im,mbc->ibc", kinetic_first, back, precision=high)
    back_rows, kinetic_rows = (
        lax.all_to_all(back, "coord", split_axis=0, concat_axis=1, tiled=True),
        lax.all_to_all(kinetic_back, "coord", split_axis=0, concat_axis=1, tiled=True),
    )
    solved = finish_slab(back_rows, basis_second, basis_third)
    kinetic = finish_slab(kinetic_rows, basis_second, basis_third)
    above = from_behind(solved, "ka", -1)
    below = from_behind(solved, "ka", 1)
    kinetic = kinetic + jnp.einsum("jm,imk->ijk", kinetic_second, solved, precision=high)
    kinetic = kinetic + jnp.einsum("km,ijm->ijk", kinetic_third, solved, precision=high)
    kval = lax.axis_index("ka").astype(jnp.float32)
    blocks = lax.axis_size("ka")
    square_top = (blocks - 1) * blocks
    coupled_up = jnp.sqrt(square_top - kval * (kval + 1.0))
    coupled_down = jnp.sqrt(square_top - (kval - 1.0) * kval)
    factor = rotation_factor[:, :, None]
    from_upper = jnp.einsum("km,ijm->ijk", coriolis_matrix, above, precision=high)
    from_lower = jnp.einsum("mk,ijm->ijk", coriolis_matrix, below, precision=high)
    coupling = factor * (coupled_up * from_upper + coupled_down * from_lower)
    applied = kinetic + (potential + kval * kval * factor) * solved + coupling
    residual = source - (applied - shift_energy * solved)
    return (solved[None], residual[None])


def solution(mesh):
    layers = mesh.shape["coord"] // 2
    plan = line_plan if layers == 4 else column_plan
    return jax.shard_map(
        plan,
        mesh=mesh,
        in_specs=(
            P("ka", "coord", None, None),
            P("coord", None, None),
            P("coord", None),
            P(),
            P(),
            P(),
            P(),
            P(),
            P(),
            P(),
            P(),
            P(),
            P(),
        ),
        out_specs=(P("ka", "coord", None, None), P("ka", "coord", None, None)),
        check_vma=False,
    )
```
